32 devices in a mesh: wall: 16 (over z, x, core), span: 2 (over y).
Axes of the slice: x: 2, y: 2, z: 4, core: 2. Of those that a mesh axis runs over, the one named last changes fastest.
Arguments:
- heat_content: float32 [192, 512, 256], P(None, 'wall', 'span'), may hold values from -6 to 6
- interval_index: int32 [192, 512, 256], P(None, 'wall', 'span'), may hold values from 0 to 15
- wall_matrix: float32 [512, 512], replicated, as said below
- base_temp: float32 [16], replicated, may hold values from -1 to 1
- enth_offset: float32 [16], replicated, may hold values from -0.5 to 0.5
- slope: float32 [16], replicated, may hold values from 0.2 to 1
- curvature: float32 [16], replicated, may hold values from 2 to 20
Outputs:
- heat_content_next: float32 [192, 512, 256], P(None, 'wall', 'span')
- thermal_state: float32 [192, 512, 256], P(None, 'wall', 'span')
The draws below stay inside these ranges and needn't reach their ends.
Inputs may be any that keep to these rules, and one draw needn't show every extreme that they name: wall_matrix[511 - i, 511 - j] = -wall_matrix[i, j] for all i, j.
All inputs are finite; a program needn't handle non-finite values.
Results may differ from the reference program's by a relative error of at most 0.0003.
Values sent between devices are 32-bit elements; how exact they have to be, the bound alone decides.
No kernel may reach another device: no remote copies, remote signals or barrier semaphores. Data moves between devices by JAX's collectives and lax.ppermute only.
A program may use at most 128 MiB of HBM per device.

```python
import math
import jax
import jax.numpy as jnp
from jax import lax

NY = 512
XP = 192
NSEG = 16
NEWTON = 4
NZ = 256


def draw_wall_matrix(key, part):
    upper_half = jax.random.normal(key, (NY // 2, NY), jnp.float32)
    upper_half = upper_half * (1.0 / NY ** 0.5)
    return jnp.concatenate([upper_half, -upper_half[::-1, ::-1]], axis=0)


def place_ends(array, stream_key, smallest, largest):
    extent = array.shape
    place = [jax.random.randint(jax.random.fold_in(stream_key, axis), (), 0, extent[axis]) for axis in range(len(extent))]
    array = array.at[tuple(place)].set(smallest)
    longest = extent.index(max(extent))
    place[longest] = (place[longest] + 1) % extent[longest]
    return array.at[tuple(place)].set(largest)


def block_scale(own_key, extent, shards, smallest, high):
    level = 1.0
    for dim, blocks in shards:
        draws = jax.random.uniform(jax.random.fold_in(jax.random.fold_in(own_key, 6), dim), (blocks,), jnp.float32, smallest / len(shards), high / len(shards))
        level = level * jnp.repeat(jnp.exp(draws), extent[dim] // blocks).reshape((-1,) + (1,) * (len(extent) - 1 - dim))
    return level


def scatter_about(key, shape, spread, limit, cuts=(), kind=jnp.bfloat16):
    entries = spread * jax.random.normal(key, shape, jnp.float32)
    if cuts:
        entries = entries * block_scale(key, shape, cuts, -0.22, 0.18)
    return jnp.clip(entries, -limit, limit).astype(kind)


def setup_inputs(seed: int = 0) -> dict:
    keys = jax.random.split(jax.random.key(seed), 8)
    return {
        "heat_content": scatter_about(keys[0], (XP, NY, NZ), 1.0, 6.0, ((1, 16), (2, 2)), jnp.float32),
        "interval_index": place_ends(jax.random.randint(keys[1], (XP, NY, NZ), 0, NSEG), jax.random.fold_in(keys[1], 1), 0, NSEG - 1).astype(jnp.int32),
        "wall_matrix": draw_wall_matrix(jax.random.fold_in(keys[7], 71), 0),
        "base_temp": jnp.clip(jax.random.uniform(keys[3], (NSEG,), jnp.float32, -1.0, 1.0), -1.0, 1.0),
        "enth_offset": jnp.clip(jax.random.uniform(keys[4], (NSEG,), jnp.float32, -0.5, 0.5), -0.5, 0.5),
        "slope": jnp.clip(jnp.exp(jax.random.uniform(keys[5], (NSEG,), jnp.float32, math.log(0.2), math.log(1.0))), 0.2, 1.0),
        "curvature": jnp.clip(jnp.exp(jax.random.uniform(keys[6], (NSEG,), jnp.float32, math.log(2.0), math.log(20.0))), 2.0, 20.0),
    }


time_step = 0.4
gamma_one = 8.0 / 15.0
gamma_two = 5.0 / 12.0
zeta_two = -17.0 / 60.0


def lookup(table, interval_index):
    indices = lax.broadcasted_iota(jnp.int32, (table.shape[0],) + interval_index.shape, 0)
    shaped = table.reshape((-1,) + (1,) * interval_index.ndim)
    return jnp.sum(jnp.where(interval_index[None] == indices, shaped, jnp.zeros_like(shaped)), axis=0)


def invert_heat_content(grid_entries, interval_lower_edge, interval_shift, first_power_factor, third_power_factor):
    remainder = grid_entries - interval_shift
    offset_temp = remainder / first_power_factor
    for sweep in range(NEWTON):
        cubic_part = third_power_factor * offset_temp * offset_temp
        mismatch = first_power_factor * offset_temp + cubic_part * offset_temp - remainder
        slope_now = first_power_factor + 3.0 * cubic_part
        offset_temp = offset_temp - mismatch / slope_now
    return interval_lower_edge + offset_temp


def heat_conductance(thermal_estimate):
    return 0.5 + 1.0 / (1.0 + thermal_estimate * thermal_estimate)


def crosswise_contribution(extended_array):
    conduct_pad = heat_conductance(extended_array)
    upper = 0.5 * (conduct_pad[..., 1:-1] + conduct_pad[..., 2:]) * (extended_array[..., 2:] - extended_array[..., 1:-1])
    lower = 0.5 * (conduct_pad[..., :-2] + conduct_pad[..., 1:-1]) * (extended_array[..., 1:-1] - extended_array[..., :-2])
    return upper - lower


def reference(heat_content, interval_index, wall_matrix, base_temp, enth_offset, slope, curvature):
    def boundary_operator(grid_entries):
        return jnp.dot(wall_matrix, grid_entries, precision=lax.Precision.HIGHEST, preferred_element_type=jnp.float32)

    def sheet_window(inputs):
        start, seg_plane = inputs
        interval_lower_edge = lookup(base_temp, seg_plane)
        interval_shift = lookup(enth_offset, seg_plane)
        first_power_factor = lookup(slope, seg_plane)
        third_power_factor = lookup(curvature, seg_plane)

        def rate(grid_entries):
            thermal_estimate = invert_heat_content(grid_entries, interval_lower_edge, interval_shift, first_power_factor, third_power_factor)
            diffusivity_factor = heat_conductance(thermal_estimate)
            spatial_derivative = boundary_operator(thermal_estimate)
            boundary_contribution = boundary_operator(diffusivity_factor * spatial_derivative)
            extended_array = jnp.concatenate([thermal_estimate[..., -1:], thermal_estimate, thermal_estimate[..., :1]], axis=-1)
            return boundary_contribution + crosswise_contribution(extended_array), thermal_estimate

        first_rate, first_temp = rate(start)
        section = start + (time_step * gamma_one) * first_rate
        second_rate, second_temp = rate(section)
        final = section + time_step * (gamma_two * second_rate + zeta_two * first_rate)
        return final, second_temp

    heat_content_next, thermal_state = lax.map(sheet_window, (heat_content, interval_index))
    return (heat_content_next, thermal_state)
```

```python
import functools

import jax
import jax.numpy as jnp
from jax import lax
from jax.experimental import pallas as pl
from jax.experimental.pallas import tpu as pltpu
from jax.sharding import PartitionSpec as P

NEWTON = 4

time_step = 0.4
gamma_one = 8.0 / 15.0
gamma_two = 5.0 / 12.0
zeta_two = -17.0 / 60.0

F32 = jnp.float32
BF16 = jnp.bfloat16
VMEM_BYTES = 48 * 1024 * 1024


def inverse(x):
    r = pl.reciprocal(x, approx=True)
    return r * (2.0 - x * r)


def lookup(row, index):
    return jnp.take_along_axis(jnp.broadcast_to(row, index.shape), index, axis=1)


def temperature(entries, index, tables):
    base = lookup(tables[0:1], index)
    shift = lookup(tables[1:2], index)
    first = lookup(tables[2:3], index)
    third = lookup(tables[3:4], index)
    remainder = entries - shift
    t = remainder * inverse(first)
    for _ in range(NEWTON):
        u = third * (t * t)
        t = (2.0 * u * t + remainder) * inverse(first + 3.0 * u)
    return base + t


def conductance(t):
    return 0.5 + inverse(1.0 + t * t)


def edge_rows(t):
    lanes = t.shape[1]
    r = lax.broadcasted_iota(jnp.int32, (8, lanes), 0)
    c = lax.broadcasted_iota(jnp.int32, (8, lanes), 1)
    pick = ((r == 0) & (c == 0)) | ((r == 1) & (c == lanes - 1))
    return lax.dot_general(
        pick.astype(F32), t, (((1,), (1,)), ((), ())),
        precision=lax.Precision.HIGHEST, preferred_element_type=F32,
    )


def edge_lanes(rows, lanes):
    r = lax.broadcasted_iota(jnp.int32, (8, lanes), 0)
    c = lax.broadcasted_iota(jnp.int32, (8, lanes), 1)
    put = ((r == 0) & (c == lanes - 1)) | ((r == 1) & (c == 0))
    return lax.dot_general(
        rows, put.astype(F32), (((0,), (0,)), ((), ())),
        precision=lax.Precision.HIGHEST, preferred_element_type=F32,
    )


def span_term(t, halo):
    lanes = t.shape[1]
    lane = lax.broadcasted_iota(jnp.int32, t.shape, 1)
    edge = edge_lanes(halo, lanes)
    c = conductance(t)
    c_edge = conductance(edge)
    low_t = jnp.where(lane == 0, edge, pltpu.roll(t, 1, 1))
    low_c = jnp.where(lane == 0, c_edge, pltpu.roll(c, 1, 1))
    high_t = jnp.where(lane == lanes - 1, edge, pltpu.roll(t, lanes - 1, 1))
    high_c = jnp.where(lane == lanes - 1, c_edge, pltpu.roll(c, lanes - 1, 1))
    return 0.5 * ((c + high_c) * (high_t - t) - (low_c + c) * (t - low_t))


def flat(ref):
    x = ref[...]
    return x.reshape(-1, x.shape[-1])


def first_kernel(h_ref, s_ref, tab_ref, t_ref, e_ref):
    t = temperature(flat(h_ref), flat(s_ref), tab_ref[...])
    t_ref[...] = t.reshape(t_ref.shape)
    e_ref[...] = edge_rows(t)


def middle_kernel(h_ref, s_ref, tab_ref, t_ref, halo_ref, wall_ref, t2_ref, part_ref, e_ref):
    h = flat(h_ref)
    rate = flat(wall_ref) + span_term(flat(t_ref), halo_ref[...])
    section = h + (time_step * gamma_one) * rate
    part = h + (time_step * (gamma_one + zeta_two)) * rate
    t2 = temperature(section, flat(s_ref), tab_ref[...])
    t2_ref[...] = t2.reshape(t2_ref.shape)
    part_ref[...] = part.reshape(part_ref.shape)
    e_ref[...] = edge_rows(t2)


def last_kernel(t_ref, halo_ref, wall_ref, part_ref, *refs):
    out_ref, state_ref = refs[-2:]
    t = flat(t_ref)
    rate = flat(wall_ref) + span_term(t, halo_ref[...])
    out = flat(part_ref) + (time_step * gamma_two) * rate
    out_ref[...] = out.reshape(out_ref.shape)
    state_ref[...] = t.reshape(state_ref.shape)


def split(x):
    hi = lax.reduce_precision(x, 8, 7).astype(BF16)
    return hi, (x - hi.astype(F32)).astype(BF16)


def apply_wall(hi, lo, x):
    x_hi, x_lo = split(x)
    dot = functools.partial(jnp.dot, preferred_element_type=F32)
    return dot(hi, x_hi) + (dot(hi, x_lo) + dot(lo, x_hi))


def wall_kernel(hi_ref, lo_ref, t_ref, out_ref):
    n, m, r, z = t_ref.shape
    hi, lo = hi_ref[...], lo_ref[...]
    step = 2 if m % 2 == 0 else 1
    for p in range(0, m, step):
        t = jnp.concatenate([t_ref[:, q].reshape(n * r, z) for q in range(p, p + step)], axis=1)
        g = apply_wall(hi, lo, t)
        w = apply_wall(hi, lo, conductance(t) * g)
        for q in range(step):
            out_ref[:, p + q] = w[:, q * z:(q + 1) * z].reshape(n, r, z)


def params():
    return pltpu.CompilerParams(vmem_limit_bytes=VMEM_BYTES)


def on_device(heat_content, interval_index, wall_matrix, base_temp, enth_offset, slope, curvature):
    planes, r, z = heat_content.shape
    n = lax.axis_size("wall")
    spans = lax.axis_size("span")
    own = planes // n
    chunks = next(k for k in (2, 3, 1) if own % k == 0)
    m = own // chunks
    h = heat_content.reshape(n, own, r, z)
    s = interval_index.reshape(n, own, r, z)
    tables = jnp.stack([base_temp, enth_offset, slope, curvature])
    tables = jnp.pad(tables, ((0, 4), (0, z - tables.shape[1])))
    w_hi, w_lo = split(wall_matrix)

    steps = next(k for k in (4, 2, 1) if n % k == 0 and (k == 1 or (n // k * m * r) % 128 == 0))
    nb = n // steps
    rows = nb * m * r
    piece = jax.ShapeDtypeStruct((n, m, r, z), F32)
    full = jax.ShapeDtypeStruct((n, own, r, z), F32)
    edges = jax.ShapeDtypeStruct((8, n * m * r), F32)
    whole_spec = lambda c: pl.BlockSpec((nb, m, r, z), lambda i: (i, c, 0, 0))
    piece_spec = pl.BlockSpec((nb, m, r, z), lambda i: (i, 0, 0, 0))
    edge_spec = pl.BlockSpec((8, rows), lambda i: (0, i))
    table_spec = pl.BlockSpec(tables.shape, lambda i: (0, 0))
    cells = n * m * r * z

    def cost(ops, arrays, flops=0):
        return pl.CostEstimate(flops=cells * ops + flops, bytes_accessed=cells * 4 * arrays, transcendentals=0)

    def first(c):
        return pl.pallas_call(
            first_kernel, grid=(steps,),
            in_specs=[whole_spec(c), whole_spec(c), table_spec],
            out_specs=[piece_spec, edge_spec], out_shape=[piece, edges],
            compiler_params=params(), cost_estimate=cost(100, 3), name="first",
        )(h, s, tables)

    def middle(c, t, halo, wall):
        return pl.pallas_call(
            middle_kernel, grid=(steps,),
            in_specs=[whole_spec(c), whole_spec(c), table_spec, piece_spec, edge_spec, piece_spec],
            out_specs=[piece_spec, piece_spec, edge_spec], out_shape=[piece, piece, edges],
            compiler_params=params(), cost_estimate=cost(140, 6), name="middle",
        )(h, s, tables, t, halo, wall)

    def last(c, t, halo, wall, part, outs):
        return pl.pallas_call(
            last_kernel, grid=(steps,),
            in_specs=[piece_spec, edge_spec, piece_spec, piece_spec] + [pl.BlockSpec(memory_space=pl.ANY)] * len(outs),
            out_specs=[whole_spec(c), whole_spec(c)], out_shape=[full, full],
            input_output_aliases={4 + i: i for i in range(len(outs))},
            compiler_params=params(), cost_estimate=cost(40, 5), name="last",
        )(t, halo, wall, part, *outs)

    def wall_operator(t):
        return pl.pallas_call(
            wall_kernel, out_shape=piece,
            in_specs=[pl.BlockSpec(memory_space=pltpu.VMEM)] * 3,
            out_specs=pl.BlockSpec(memory_space=pltpu.VMEM),
            compiler_params=params(), cost_estimate=cost(20, 3, 12 * n * r * cells), name="wall",
        )(w_hi, w_lo, t)

    def exchange(x):
        return lax.all_to_all(x, "wall", split_axis=0, concat_axis=0, tiled=True)

    def neighbours(e):
        forward = [(i, (i + 1) % spans) for i in range(spans)]
        if spans == 2:
            return lax.ppermute(e, "span", forward)
        backward = [(target, source) for source, target in forward]
        up = lax.ppermute(e[0:1], "span", backward)
        down = lax.ppermute(e[1:2], "span", forward)
        return jnp.concatenate([up, down, jnp.zeros_like(e[2:])], axis=0)

    parts, outs = [], ()
    started = [first(c) for c in range(chunks)]
    state = []
    for t, e in started:
        state.append((t, neighbours(e), exchange(t)))
    state = [(t, halo, exchange(wall_operator(g))) for t, halo, g in state]
    nxt = []
    for c, (t, halo, w) in enumerate(state):
        t2, part, e2 = middle(c, t, halo, w)
        nxt.append((t2, part, neighbours(e2), exchange(t2)))
    nxt = [(t, part, halo, exchange(wall_operator(g))) for t, part, halo, g in nxt]
    for c, (t, part, halo, w) in enumerate(nxt):
        outs = last(c, t, halo, w, part, outs)
    return outs[0].reshape(planes, r, z), outs[1].reshape(planes, r, z)


def solution(mesh):
    in_specs = (P(None, "wall", "span"), P(None, "wall", "span"), P(), P(), P(), P(), P())
    out_specs = (P(None, "wall", "span"), P(None, "wall", "span"))
    return jax.shard_map(
        on_device, mesh=mesh, in_specs=in_specs, out_specs=out_specs, check_vma=False
    )
```

```python
import functools

import jax
import jax.numpy as jnp
from jax import lax
from jax.experimental import pallas as pl
from jax.experimental.pallas import tpu as pltpu
from jax.sharding import PartitionSpec as P

NEWTON = 4

time_step = 0.4
gamma_one = 8.0 / 15.0
gamma_two = 5.0 / 12.0
zeta_two = -17.0 / 60.0

F32 = jnp.float32
BF16 = jnp.bfloat16
VMEM_BYTES = 24 * 1024 * 1024
CHUNKS = (2, 3, 1)
ORDER = (4, 2, 7, 1, 6, 5, 3)
WINDOW = 4
EARLY = 6


def inverse(x):
    r = pl.reciprocal(x, approx=True)
    return r * (2.0 - x * r)


def lookup(row, index):
    return jnp.take_along_axis(jnp.broadcast_to(row, index.shape), index, axis=1)


def temperature(entries, index, tables):
    base = lookup(tables[0:1], index)
    shift = lookup(tables[1:2], index)
    first = lookup(tables[2:3], index)
    third = lookup(tables[3:4], index)
    remainder = entries - shift
    t = remainder * inverse(first)
    for _ in range(NEWTON):
        u = third * (t * t)
        t = (2.0 * u * t + remainder) * inverse(first + 3.0 * u)
    return base + t


def conductance(t):
    return 0.5 + inverse(1.0 + t * t)


def edge_rows(t):
    lanes = t.shape[1]
    r = lax.broadcasted_iota(jnp.int32, (8, lanes), 0)
    c = lax.broadcasted_iota(jnp.int32, (8, lanes), 1)
    pick = ((r == 0) & (c == 0)) | ((r == 1) & (c == lanes - 1))
    return lax.dot_general(
        pick.astype(F32), t, (((1,), (1,)), ((), ())),
        precision=lax.Precision.HIGHEST, preferred_element_type=F32,
    )


def edge_lanes(rows, lanes):
    r = lax.broadcasted_iota(jnp.int32, (8, lanes), 0)
    c = lax.broadcasted_iota(jnp.int32, (8, lanes), 1)
    put = ((r == 0) & (c == lanes - 1)) | ((r == 1) & (c == 0))
    return lax.dot_general(
        rows, put.astype(F32), (((0,), (0,)), ((), ())),
        precision=lax.Precision.HIGHEST, preferred_element_type=F32,
    )


def span_term(t, halo):
    lanes = t.shape[1]
    lane = lax.broadcasted_iota(jnp.int32, t.shape, 1)
    edge = edge_lanes(halo, lanes)
    c = conductance(t)
    c_edge = conductance(edge)
    low_t = jnp.where(lane == 0, edge, pltpu.roll(t, 1, 1))
    low_c = jnp.where(lane == 0, c_edge, pltpu.roll(c, 1, 1))
    high_t = jnp.where(lane == lanes - 1, edge, pltpu.roll(t, lanes - 1, 1))
    high_c = jnp.where(lane == lanes - 1, c_edge, pltpu.roll(c, lanes - 1, 1))
    return 0.5 * ((c + high_c) * (high_t - t) - (low_c + c) * (t - low_t))


def spread(ref):
    return ref[...].reshape(-1, ref.shape[-1])


def fetched(me_ref, ref):
    chip, core = me_ref[0], me_ref[1]
    return jnp.concatenate(
        [ref[chip ^ p, core ^ q, 0] for q in range(2) for p in range(ref.shape[0])], axis=0
    )


def store(same_ref, other_ref, x):
    half = x.shape[0] // 2
    same_ref[...] = x[:half].reshape(same_ref.shape)
    other_ref[...] = x[half:].reshape(other_ref.shape)


def first_kernel(me_ref, h_ref, s_ref, tab_ref, same_ref, other_ref, e_ref):
    t = temperature(fetched(me_ref, h_ref), fetched(me_ref, s_ref), tab_ref[...])
    store(same_ref, other_ref, t)
    e_ref[0] = edge_rows(t)


def rate_of(t, halo_ref, crossed_ref, back_refs):
    wall = jnp.concatenate([spread(ref) for ref in back_refs] + [spread(crossed_ref)], axis=0)
    return wall + span_term(t, halo_ref[0])


def middle_kernel(chips, me_ref, h_ref, s_ref, tab_ref, same_ref, other_ref, halo_ref, crossed_ref, *refs):
    back_refs, (same2_ref, other2_ref, part_ref, e_ref) = refs[:chips], refs[chips:]
    h = fetched(me_ref, h_ref)
    t = jnp.concatenate([spread(same_ref), spread(other_ref)], axis=0)
    rate = rate_of(t, halo_ref, crossed_ref, back_refs)
    section = h + (time_step * gamma_one) * rate
    part_ref[...] = (h + (time_step * (gamma_one + zeta_two)) * rate).reshape(part_ref.shape)
    t2 = temperature(section, fetched(me_ref, s_ref), tab_ref[...])
    store(same2_ref, other2_ref, t2)
    e_ref[0] = edge_rows(t2)


def last_kernel(chips, me_ref, same_ref, other_ref, halo_ref, part_ref, crossed_ref, *refs):
    back_refs = refs[:chips]
    out_ref, state_ref = refs[-2:]
    t = jnp.concatenate([spread(same_ref), spread(other_ref)], axis=0)
    rate = rate_of(t, halo_ref, crossed_ref, back_refs)
    out = part_ref[...].reshape(t.shape) + (time_step * gamma_two) * rate
    chip, core = me_ref[0], me_ref[1]
    r = out_ref.shape[-2]
    for q in range(2):
        for p in range(chips):
            at = (q * chips + p) * r
            out_ref[chip ^ p, core ^ q, 0] = out[at:at + r]
            state_ref[chip ^ p, core ^ q, 0] = t[at:at + r]


def pair_kernel(same_ref, crossed_ref, *outs):
    for p, out in enumerate(outs, 1):
        out[0] = same_ref[p]
        out[1] = crossed_ref[p]


def gather_kernel(*refs):
    for p, ref in enumerate(refs[:-1]):
        refs[-1][p] = ref[0]


def split(x):
    hi = lax.reduce_precision(x, 8, 7).astype(BF16)
    return hi, (x - hi.astype(F32)).astype(BF16)


def apply_wall(hi, lo, x):
    x_hi, x_lo = split(x)
    dot = functools.partial(jnp.dot, preferred_element_type=F32)
    return dot(hi, x_hi) + (dot(hi, x_lo) + dot(lo, x_hi))


def wall_kernel(chips, me_ref, hi_ref, lo_ref, same_ref, crossed_ref, *refs):
    moved, outs, hold = refs[:chips - 1], refs[chips - 1:-1], refs[-1]
    n, m, r, z = hold.shape
    chip, core = me_ref[0], me_ref[1]
    for q in range(2):
        hold[chip * 2 + (core ^ q)] = (same_ref, crossed_ref)[q][0]
        for p in range(1, chips):
            hold[(chip ^ p) * 2 + (core ^ q)] = moved[p - 1][q]
    hi, lo = hi_ref[...], lo_ref[...]
    t = jnp.concatenate([hold[:, k].reshape(n * r, z) for k in range(m)], axis=1)
    g = apply_wall(hi, lo, t)
    w = apply_wall(hi, lo, conductance(t) * g)
    for k in range(m):
        hold[:, k] = w[:, k * z:(k + 1) * z].reshape(n, r, z)
    for q in range(2):
        for p in range(chips):
            outs[p][q] = hold[(chip ^ p) * 2 + (core ^ q)]


def params():
    return pltpu.CompilerParams(vmem_limit_bytes=VMEM_BYTES)


def on_device(heat_content, interval_index, wall_matrix, base_temp, enth_offset, slope, curvature):
    planes, r, z = heat_content.shape
    n = lax.axis_size("wall")
    spans = lax.axis_size("span")
    chips = n // 2
    own = planes // n
    chunks = next(k for k in CHUNKS if own % k == 0)
    m = own // chunks
    order = ORDER if chips == 8 else list(range(1, chips))
    index = lax.axis_index("wall")
    me = jnp.stack([index // 2, index % 2]).astype(jnp.int32)
    h = heat_content.reshape(chips, 2, own, r, z)
    s = interval_index.reshape(chips, 2, own, r, z)
    tables = jnp.stack([base_temp, enth_offset, slope, curvature])
    tables = jnp.pad(tables, ((0, 4), (0, z - tables.shape[1])))
    w_hi, w_lo = split(wall_matrix)

    half = jax.ShapeDtypeStruct((chips, m, r, z), F32)
    pair = jax.ShapeDtypeStruct((2, m, r, z), F32)
    both = jax.ShapeDtypeStruct((2, chips, m, r, z), F32)
    full = jax.ShapeDtypeStruct((chips, 2, own, r, z), F32)
    edges = jax.ShapeDtypeStruct((m, 8, n * r), F32)
    whole_spec = lambda c: pl.BlockSpec((chips, 2, 1, r, z), lambda i, me: (0, 0, c * m + i, 0, 0))
    half_spec = pl.BlockSpec((chips, 1, r, z), lambda i, me: (0, i, 0, 0))
    back_spec = pl.BlockSpec((1, 1, r, z), lambda i, me: (0, i, 0, 0))
    both_spec = pl.BlockSpec((2, chips, 1, r, z), lambda i, me: (0, 0, i, 0, 0))
    edge_spec = pl.BlockSpec((1, 8, n * r), lambda i, me: (i, 0, 0))
    table_spec = pl.BlockSpec(tables.shape, lambda i, me: (0, 0))
    hbm = pl.BlockSpec(memory_space=pl.ANY)
    cells = n * m * r * z

    def cost(ops, arrays, flops=0):
        return pl.CostEstimate(flops=cells * ops + flops, bytes_accessed=cells * 4 * arrays, transcendentals=0)

    def call(kernel, ins, outs, shapes, estimate, name, aliases={}, scratch=(), steps=m):
        grid = pltpu.PrefetchScalarGridSpec(
            num_scalar_prefetch=1, grid=(steps,), in_specs=ins, out_specs=outs, scratch_shapes=scratch
        )
        return pl.pallas_call(
            kernel, grid_spec=grid, out_shape=shapes, input_output_aliases=aliases,
            compiler_params=params(), cost_estimate=estimate, name=name,
        )

    def first(c, me):
        return call(
            first_kernel, [whole_spec(c), whole_spec(c), table_spec], [half_spec, half_spec, edge_spec],
            [half, half, edges], cost(100, 3), "first",
        )(me, h, s, tables)

    def middle(c, same, other, halo, crossed, back):
        return call(
            functools.partial(middle_kernel, chips),
            [whole_spec(c), whole_spec(c), table_spec, half_spec, half_spec, edge_spec, half_spec] + [back_spec] * chips,
            [half_spec, half_spec, both_spec, edge_spec], [half, half, both, edges], cost(140, 6), "middle",
        )(me, h, s, tables, same, other, halo, crossed, *back)

    def last(c, same, other, halo, part, crossed, back, outs):
        return call(
            functools.partial(last_kernel, chips),
            [half_spec, half_spec, edge_spec, both_spec, half_spec] + [back_spec] * chips + [hbm] * len(outs),
            [whole_spec(c)] * 2, [full] * 2, cost(40, 5), "last",
            {6 + chips + i: i for i in range(len(outs))},
        )(me, same, other, halo, part, crossed, *back, *outs)

    def block(shape, at=0):
        return pl.BlockSpec(shape, lambda i, me: (at,) + (0,) * (len(shape) - 1))

    def wall_operator(same, crossed, moved):
        return call(
            functools.partial(wall_kernel, chips),
            [block(w_hi.shape)] * 2 + [block((1, m, r, z))] * 2 + [block(pair.shape)] * (chips - 1),
            [block(pair.shape)] * chips, [pair] * chips, cost(20, 3, 12 * n * r * cells), "wall",
            scratch=[pltpu.VMEM((n, m, r, z), F32)], steps=1,
        )(me, w_hi, w_lo, same, crossed, *moved)

    def pairs(same, crossed):
        vmem = pl.BlockSpec(memory_space=pltpu.VMEM)
        return pl.pallas_call(
            pair_kernel, out_shape=[pair] * (chips - 1), in_specs=[vmem] * 2, out_specs=[vmem] * (chips - 1),
            compiler_params=params(), cost_estimate=cost(1, 2), name="pairs",
        )(same, crossed)

    def gather(back):
        return pl.pallas_call(
            gather_kernel, grid=(1,), out_shape=half,
            in_specs=[pl.BlockSpec((1, m, r, z), lambda i: (1, 0, 0, 0))] * chips,
            out_specs=pl.BlockSpec(half.shape, lambda i: (0, 0, 0, 0)),
            compiler_params=params(), cost_estimate=cost(1, 1), name="gather",
        )(*back)

    sent = []

    def after(x, tokens):
        return lax.optimization_barrier((x, *tokens))[0] if tokens else x

    def between_chips(arrays, places, tokens=()):
        moved = {}
        for p in (order[k] for k in places):
            x = after(arrays[p - 1], tuple(sent[-WINDOW:][:1] if len(sent) >= WINDOW else ()) + tuple(tokens))
            moved[p] = lax.ppermute(x, "wall", [(i, i ^ (2 * p)) for i in range(n)])
            sent.append(moved[p])
            tokens = ()
        return moved

    def between_cores(x):
        return lax.ppermute(x, "wall", [(i, i ^ 1) for i in range(n)])

    def neighbours(e):
        forward = [(i, (i + 1) % spans) for i in range(spans)]
        if spans == 2:
            return lax.ppermute(e, "span", forward)
        backward = [(target, source) for source, target in forward]
        up = lax.ppermute(e[:, 0:1], "span", backward)
        down = lax.ppermute(e[:, 1:2], "span", forward)
        return jnp.concatenate([up, down, jnp.zeros_like(e[:, 2:])], axis=1)

    chunk = [dict() for _ in range(chunks)]
    outs = ()

    def start_first(c, tokens):
        d = chunk[c]
        d["same"], d["other"], e = first(c, after(me, tokens))
        d["crossed"] = between_cores(d["other"])
        d["halo"] = neighbours(e)
        d["send"] = pairs(d["same"], d["crossed"])
        return d["same"]

    def produce(c, phase, tokens=()):
        nonlocal outs
        d = chunk[c]
        moved = [d["moved"][p] for p in range(1, chips)]
        if phase in (1, 3):
            w = wall_operator(d["same"], after(d["crossed"], tokens), moved)
            d["own"], d["send"] = w[0], w[1:]
            return w[0]
        back = [d["own"]] + moved
        crossed = after(between_cores(gather(back)), tokens)
        if phase == 2:
            d["same"], d["other"], d["part"], e = middle(c, d["same"], d["other"], d["halo"], crossed, back)
            d["crossed"] = between_cores(d["other"])
            d["halo"] = neighbours(e)
            d["send"] = pairs(d["same"], d["crossed"])
            return d["same"]
        outs = last(c, d["same"], d["other"], d["halo"], d["part"], crossed, back, outs)
        return outs[0]

    start_first(0, ())
    early = min(EARLY, len(order))
    for j in range(4 * chunks):
        phase, c = divmod(j, chunks)
        d = chunk[c]
        tokens = []
        d["moved"] = between_chips(d["send"], range(early))
        if j + 1 < chunks:
            tokens.append(start_first(j + 1, (d["send"][order[0] - 1],)))
        if j >= 1:
            before, k = divmod(j - 1, chunks)
            tokens.append(produce(k, before + 1))
        late = list(range(early, len(order)))
        d["moved"].update(between_chips(d["send"], late[:-1], tokens))
        d["moved"].update(between_chips(d["send"], late[-1:], (d["halo"],) if phase in (0, 2) else ()))
    produce(chunks - 1, 4)
    return outs[0].reshape(planes, r, z), outs[1].reshape(planes, r, z)


def solution(mesh):
    in_specs = (P(None, "wall", "span"), P(None, "wall", "span"), P(), P(), P(), P(), P())
    out_specs = (P(None, "wall", "span"), P(None, "wall", "span"))
    return jax.shard_map(
        on_device, mesh=mesh, in_specs=in_specs, out_specs=out_specs, check_vma=False
    )
```

```python
import functools

import jax
import jax.numpy as jnp
from jax import lax
from jax.experimental import pallas as pl
from jax.experimental.pallas import tpu as pltpu
from jax.sharding import PartitionSpec as P

NEWTON = 4

time_step = 0.4
gamma_one = 8.0 / 15.0
gamma_two = 5.0 / 12.0
zeta_two = -17.0 / 60.0

F32 = jnp.float32
BF16 = jnp.bfloat16
VMEM_BYTES = 24 * 1024 * 1024
CHUNKS = (2, 3, 1)
ORDER = (4, 7, 2, 6, 1, 5, 3)
WINDOW = 4
EARLY = 4


def inverse(x):
    r = pl.reciprocal(x, approx=True)
    return r * (2.0 - x * r)


def lookup(row, index):
    return jnp.take_along_axis(jnp.broadcast_to(row, index.shape), index, axis=1)


def temperature(entries, index, tables):
    base = lookup(tables[0:1], index)
    shift = lookup(tables[1:2], index)
    first = lookup(tables[2:3], index)
    third = lookup(tables[3:4], index)
    remainder = entries - shift
    t = remainder * inverse(first)
    for _ in range(NEWTON):
        u = third * (t * t)
        t = (2.0 * u * t + remainder) * inverse(first + 3.0 * u)
    return base + t


def conductance(t):
    return 0.5 + inverse(1.0 + t * t)


def edge_rows(t):
    lanes = t.shape[1]
    r = lax.broadcasted_iota(jnp.int32, (8, lanes), 0)
    c = lax.broadcasted_iota(jnp.int32, (8, lanes), 1)
    pick = ((r == 0) & (c == 0)) | ((r == 1) & (c == lanes - 1))
    return lax.dot_general(
        pick.astype(F32), t, (((1,), (1,)), ((), ())),
        precision=lax.Precision.HIGHEST, preferred_element_type=F32,
    )


def edge_lanes(rows, lanes):
    r = lax.broadcasted_iota(jnp.int32, (8, lanes), 0)
    c = lax.broadcasted_iota(jnp.int32, (8, lanes), 1)
    put = ((r == 0) & (c == lanes - 1)) | ((r == 1) & (c == 0))
    return lax.dot_general(
        rows, put.astype(F32), (((0,), (0,)), ((), ())),
        precision=lax.Precision.HIGHEST, preferred_element_type=F32,
    )


def span_term(t, halo):
    lanes = t.shape[1]
    lane = lax.broadcasted_iota(jnp.int32, t.shape, 1)
    edge = edge_lanes(halo, lanes)
    c = conductance(t)
    c_edge = conductance(edge)
    low_t = jnp.where(lane == 0, edge, pltpu.roll(t, 1, 1))
    low_c = jnp.where(lane == 0, c_edge, pltpu.roll(c, 1, 1))
    high_t = jnp.where(lane == lanes - 1, edge, pltpu.roll(t, lanes - 1, 1))
    high_c = jnp.where(lane == lanes - 1, c_edge, pltpu.roll(c, lanes - 1, 1))
    return 0.5 * ((c + high_c) * (high_t - t) - (low_c + c) * (t - low_t))


def spread(ref):
    return ref[...].reshape(-1, ref.shape[-1])


def fetched(me_ref, ref):
    chip, core = me_ref[0], me_ref[1]
    return jnp.concatenate(
        [ref[chip ^ p, core ^ q, 0] for q in range(2) for p in range(ref.shape[0])], axis=0
    )


def store(same_ref, other_ref, x):
    half = x.shape[0] // 2
    same_ref[...] = x[:half].reshape(same_ref.shape)
    other_ref[...] = x[half:].reshape(other_ref.shape)


def first_kernel(me_ref, h_ref, s_ref, tab_ref, same_ref, other_ref, e_ref):
    t = temperature(fetched(me_ref, h_ref), fetched(me_ref, s_ref), tab_ref[...])
    store(same_ref, other_ref, t)
    e_ref[0] = edge_rows(t)


def rate_of(t, halo_ref, crossed_ref, back_refs):
    wall = jnp.concatenate([spread(ref) for ref in back_refs] + [spread(crossed_ref)], axis=0)
    return wall + span_term(t, halo_ref[0])


def middle_kernel(chips, me_ref, h_ref, s_ref, tab_ref, same_ref, other_ref, halo_ref, crossed_ref, *refs):
    back_refs, (same2_ref, other2_ref, part_ref, e_ref) = refs[:chips], refs[chips:]
    h = fetched(me_ref, h_ref)
    t = jnp.concatenate([spread(same_ref), spread(other_ref)], axis=0)
    rate = rate_of(t, halo_ref, crossed_ref, back_refs)
    section = h + (time_step * gamma_one) * rate
    part_ref[...] = (h + (time_step * (gamma_one + zeta_two)) * rate).reshape(part_ref.shape)
    t2 = temperature(section, fetched(me_ref, s_ref), tab_ref[...])
    store(same2_ref, other2_ref, t2)
    e_ref[0] = edge_rows(t2)


def last_kernel(chips, me_ref, same_ref, other_ref, halo_ref, part_ref, crossed_ref, *refs):
    back_refs = refs[:chips]
    out_ref, state_ref = refs[-2:]
    t = jnp.concatenate([spread(same_ref), spread(other_ref)], axis=0)
    rate = rate_of(t, halo_ref, crossed_ref, back_refs)
    out = part_ref[...].reshape(t.shape) + (time_step * gamma_two) * rate
    chip, core = me_ref[0], me_ref[1]
    r = out_ref.shape[-2]
    for q in range(2):
        for p in range(chips):
            at = (q * chips + p) * r
            out_ref[chip ^ p, core ^ q, 0] = out[at:at + r]
            state_ref[chip ^ p, core ^ q, 0] = t[at:at + r]


def pair_kernel(same_ref, crossed_ref, *outs):
    for p, out in enumerate(outs, 1):
        out[0] = same_ref[p]
        out[1] = crossed_ref[p]


def gather_kernel(*refs):
    for p, ref in enumerate(refs[:-1]):
        refs[-1][p] = ref[0]


def split(x):
    hi = lax.reduce_precision(x, 8, 7).astype(BF16)
    return hi, (x - hi.astype(F32)).astype(BF16)


def apply_wall(hi, lo, x):
    x_hi, x_lo = split(x)
    dot = functools.partial(jnp.dot, preferred_element_type=F32)
    return dot(hi, x_hi) + (dot(hi, x_lo) + dot(lo, x_hi))


def wall_kernel(chips, me_ref, hi_ref, lo_ref, same_ref, crossed_ref, *refs):
    moved, outs, hold = refs[:chips - 1], refs[chips - 1:-1], refs[-1]
    n, m, r, z = hold.shape
    chip, core = me_ref[0], me_ref[1]
    for q in range(2):
        hold[chip * 2 + (core ^ q)] = (same_ref, crossed_ref)[q][0]
        for p in range(1, chips):
            hold[(chip ^ p) * 2 + (core ^ q)] = moved[p - 1][q]
    hi, lo = hi_ref[...], lo_ref[...]
    t = jnp.concatenate([hold[:, k].reshape(n * r, z) for k in range(m)], axis=1)
    g = apply_wall(hi, lo, t)
    w = apply_wall(hi, lo, conductance(t) * g)
    for k in range(m):
        hold[:, k] = w[:, k * z:(k + 1) * z].reshape(n, r, z)
    for q in range(2):
        for p in range(chips):
            outs[p][q] = hold[(chip ^ p) * 2 + (core ^ q)]


def params():
    return pltpu.CompilerParams(vmem_limit_bytes=VMEM_BYTES)


def on_device(heat_content, interval_index, wall_matrix, base_temp, enth_offset, slope, curvature):
    planes, r, z = heat_content.shape
    n = lax.axis_size("wall")
    spans = lax.axis_size("span")
    chips = n // 2
    own = planes // n
    chunks = next(k for k in CHUNKS if own % k == 0)
    m = own // chunks
    order = ORDER if chips == 8 else list(range(1, chips))
    index = lax.axis_index("wall")
    me = jnp.stack([index // 2, index % 2]).astype(jnp.int32)
    h = heat_content.reshape(chips, 2, own, r, z)
    s = interval_index.reshape(chips, 2, own, r, z)
    tables = jnp.stack([base_temp, enth_offset, slope, curvature])
    tables = jnp.pad(tables, ((0, 4), (0, z - tables.shape[1])))
    w_hi, w_lo = split(wall_matrix)

    half = jax.ShapeDtypeStruct((chips, m, r, z), F32)
    pair = jax.ShapeDtypeStruct((2, m, r, z), F32)
    both = jax.ShapeDtypeStruct((2, chips, m, r, z), F32)
    full = jax.ShapeDtypeStruct((chips, 2, own, r, z), F32)
    edges = jax.ShapeDtypeStruct((m, 8, n * r), F32)
    whole_spec = lambda c: pl.BlockSpec((chips, 2, 1, r, z), lambda i, me: (0, 0, c * m + i, 0, 0))
    half_spec = pl.BlockSpec((chips, 1, r, z), lambda i, me: (0, i, 0, 0))
    back_spec = pl.BlockSpec((1, 1, r, z), lambda i, me: (0, i, 0, 0))
    both_spec = pl.BlockSpec((2, chips, 1, r, z), lambda i, me: (0, 0, i, 0, 0))
    edge_spec = pl.BlockSpec((1, 8, n * r), lambda i, me: (i, 0, 0))
    table_spec = pl.BlockSpec(tables.shape, lambda i, me: (0, 0))
    hbm = pl.BlockSpec(memory_space=pl.ANY)
    cells = n * m * r * z

    def cost(ops, arrays, flops=0):
        return pl.CostEstimate(flops=1, bytes_accessed=1, transcendentals=0)

    def call(kernel, ins, outs, shapes, estimate, name, aliases={}, scratch=(), steps=m):
        grid = pltpu.PrefetchScalarGridSpec(
            num_scalar_prefetch=1, grid=(steps,), in_specs=ins, out_specs=outs, scratch_shapes=scratch
        )
        return pl.pallas_call(
            kernel, grid_spec=grid, out_shape=shapes, input_output_aliases=aliases,
            compiler_params=params(), cost_estimate=estimate, name=name,
        )

    def first(c, me):
        return call(
            first_kernel, [whole_spec(c), whole_spec(c), table_spec], [half_spec, half_spec, edge_spec],
            [half, half, edges], cost(100, 3), "first",
        )(me, h, s, tables)

    def middle(c, same, other, halo, crossed, back):
        return call(
            functools.partial(middle_kernel, chips),
            [whole_spec(c), whole_spec(c), table_spec, half_spec, half_spec, edge_spec, half_spec] + [back_spec] * chips,
            [half_spec, half_spec, both_spec, edge_spec], [half, half, both, edges], cost(140, 6), "middle",
        )(me, h, s, tables, same, other, halo, crossed, *back)

    def last(c, same, other, halo, part, crossed, back, outs):
        return call(
            functools.partial(last_kernel, chips),
            [half_spec, half_spec, edge_spec, both_spec, half_spec] + [back_spec] * chips + [hbm] * len(outs),
            [whole_spec(c)] * 2, [full] * 2, cost(40, 5), "last",
            {6 + chips + i: i for i in range(len(outs))},
        )(me, same, other, halo, part, crossed, *back, *outs)

    def block(shape, at=0):
        return pl.BlockSpec(shape, lambda i, me: (at,) + (0,) * (len(shape) - 1))

    def wall_operator(same, crossed, moved):
        return call(
            functools.partial(wall_kernel, chips),
            [block(w_hi.shape)] * 2 + [block((1, m, r, z))] * 2 + [block(pair.shape)] * (chips - 1),
            [block(pair.shape)] * chips, [pair] * chips, cost(20, 3, 12 * n * r * cells), "wall",
            scratch=[pltpu.VMEM((n, m, r, z), F32)], steps=1,
        )(me, w_hi, w_lo, same, crossed, *moved)

    def pairs(same, crossed):
        vmem = pl.BlockSpec(memory_space=pltpu.VMEM)
        return pl.pallas_call(
            pair_kernel, out_shape=[pair] * (chips - 1), in_specs=[vmem] * 2, out_specs=[vmem] * (chips - 1),
            compiler_params=params(), cost_estimate=cost(1, 2), name="pairs",
        )(same, crossed)

    def gather(back):
        return pl.pallas_call(
            gather_kernel, grid=(1,), out_shape=half,
            in_specs=[pl.BlockSpec((1, m, r, z), lambda i: (1, 0, 0, 0))] * chips,
            out_specs=pl.BlockSpec(half.shape, lambda i: (0, 0, 0, 0)),
            compiler_params=params(), cost_estimate=cost(1, 1), name="gather",
        )(*back)

    sent = []

    def after(x, tokens):
        return lax.optimization_barrier((x, *tokens))[0] if tokens else x

    def between_chips(arrays, places, tokens=()):
        moved = {}
        for p in (order[k] for k in places):
            x = after(arrays[p - 1], tuple(sent[-WINDOW:][:1] if len(sent) >= WINDOW else ()) + tuple(tokens))
            moved[p] = lax.ppermute(x, "wall", [(i, i ^ (2 * p)) for i in range(n)])
            sent.append(moved[p])
            tokens = ()
        return moved

    def between_cores(x):
        return lax.ppermute(x, "wall", [(i, i ^ 1) for i in range(n)])

    def neighbours(e):
        forward = [(i, (i + 1) % spans) for i in range(spans)]
        if spans == 2:
            return lax.ppermute(e, "span", forward)
        backward = [(target, source) for source, target in forward]
        up = lax.ppermute(e[:, 0:1], "span", backward)
        down = lax.ppermute(e[:, 1:2], "span", forward)
        return jnp.concatenate([up, down, jnp.zeros_like(e[:, 2:])], axis=1)

    chunk = [dict() for _ in range(chunks)]
    outs = ()

    def start_first(c, tokens):
        d = chunk[c]
        d["same"], d["other"], e = first(c, after(me, tokens))
        d["crossed"] = between_cores(d["other"])
        d["halo"] = neighbours(e)
        d["send"] = pairs(d["same"], d["crossed"])
        return d["same"]

    def produce(c, phase, tokens=()):
        nonlocal outs
        d = chunk[c]
        moved = [d["moved"][p] for p in range(1, chips)]
        if phase in (1, 3):
            w = wall_operator(d["same"], after(d["crossed"], tokens), moved)
            d["own"], d["send"] = w[0], w[1:]
            return w[0]
        back = [d["own"]] + moved
        crossed = after(between_cores(gather(back)), tokens)
        if phase == 2:
            d["same"], d["other"], d["part"], e = middle(c, d["same"], d["other"], d["halo"], crossed, back)
            d["crossed"] = between_cores(d["other"])
            d["halo"] = neighbours(e)
            d["send"] = pairs(d["same"], d["crossed"])
            return d["same"]
        outs = last(c, d["same"], d["other"], d["halo"], d["part"], crossed, back, outs)
        return outs[0]

    start_first(0, ())
    early = min(EARLY, len(order))
    for j in range(4 * chunks):
        phase, c = divmod(j, chunks)
        d = chunk[c]
        tokens = []
        d["moved"] = between_chips(d["send"], range(early))
        if j + 1 < chunks:
            tokens.append(start_first(j + 1, (d["send"][order[0] - 1],)))
        if j >= 1:
            before, k = divmod(j - 1, chunks)
            tokens.append(produce(k, before + 1))
        late = list(range(early, len(order)))
        d["moved"].update(between_chips(d["send"], late[:-1], tokens))
        d["moved"].update(between_chips(d["send"], late[-1:], (d["halo"],) if phase in (0, 2) else ()))
    produce(chunks - 1, 4)
    return outs[0].reshape(planes, r, z), outs[1].reshape(planes, r, z)


def solution(mesh):
    in_specs = (P(None, "wall", "span"), P(None, "wall", "span"), P(), P(), P(), P(), P())
    out_specs = (P(None, "wall", "span"), P(None, "wall", "span"))
    return jax.shard_map(
        on_device, mesh=mesh, in_specs=in_specs, out_specs=out_specs, check_vma=False
    )
```

```python
import functools

import jax
import jax.numpy as jnp
from jax import lax
from jax.experimental import pallas as pl
from jax.experimental.pallas import tpu as pltpu
from jax.sharding import PartitionSpec as P

NEWTON = 4

time_step = 0.4
gamma_one = 8.0 / 15.0
gamma_two = 5.0 / 12.0
zeta_two = -17.0 / 60.0

F32 = jnp.float32
BF16 = jnp.bfloat16
VMEM_BYTES = 24 * 1024 * 1024
CHUNKS = (2, 3, 1)
ORDER = (4, 7, 2, 6, 1, 5, 3)
WINDOW = 4
EARLY = 4


def inverse(x):
    r = pl.reciprocal(x, approx=True)
    return r * (2.0 - x * r)


def lookup(row, index):
    return jnp.take_along_axis(jnp.broadcast_to(row, index.shape), index, axis=1)


def temperature(entries, index, tables):
    base = lookup(tables[0:1], index)
    shift = lookup(tables[1:2], index)
    first = lookup(tables[2:3], index)
    third = lookup(tables[3:4], index)
    remainder = entries - shift
    t = remainder * inverse(first)
    triple = 3.0 * third
    double = 2.0 * third
    for _ in range(NEWTON):
        square = t * t
        t = (double * square * t + remainder) * inverse(first + triple * square)
    return base + t


def conductance(t):
    return 0.5 + inverse(1.0 + t * t)


def edge_rows(t):
    lanes = t.shape[1]
    r = lax.broadcasted_iota(jnp.int32, (8, lanes), 0)
    c = lax.broadcasted_iota(jnp.int32, (8, lanes), 1)
    pick = ((r == 0) & (c == 0)) | ((r == 1) & (c == lanes - 1))
    return lax.dot_general(
        pick.astype(F32), t, (((1,), (1,)), ((), ())),
        precision=lax.Precision.HIGHEST, preferred_element_type=F32,
    )


def edge_lanes(rows, lanes):
    r = lax.broadcasted_iota(jnp.int32, (8, lanes), 0)
    c = lax.broadcasted_iota(jnp.int32, (8, lanes), 1)
    put = ((r == 0) & (c == lanes - 1)) | ((r == 1) & (c == 0))
    return lax.dot_general(
        rows, put.astype(F32), (((0,), (0,)), ((), ())),
        precision=lax.Precision.HIGHEST, preferred_element_type=F32,
    )


def span_term(t, halo):
    lanes = t.shape[1]
    lane = lax.broadcasted_iota(jnp.int32, t.shape, 1)
    edge = edge_lanes(halo, lanes)
    c = conductance(t)
    c_edge = conductance(edge)
    low_t = jnp.where(lane == 0, edge, pltpu.roll(t, 1, 1))
    low_c = jnp.where(lane == 0, c_edge, pltpu.roll(c, 1, 1))
    high_t = jnp.where(lane == lanes - 1, edge, pltpu.roll(t, lanes - 1, 1))
    high_c = jnp.where(lane == lanes - 1, c_edge, pltpu.roll(c, lanes - 1, 1))
    return 0.5 * ((c + high_c) * (high_t - t) - (low_c + c) * (t - low_t))


def spread(ref):
    return ref[...].reshape(-1, ref.shape[-1])


def fetched(me_ref, ref):
    chip, core = me_ref[0], me_ref[1]
    return jnp.concatenate(
        [ref[chip ^ p, core ^ q, 0] for q in range(2) for p in range(ref.shape[0])], axis=0
    )


def store(same_ref, other_ref, x):
    half = x.shape[0] // 2
    same_ref[...] = x[:half].reshape(same_ref.shape)
    other_ref[...] = x[half:].reshape(other_ref.shape)


def first_kernel(me_ref, h_ref, s_ref, tab_ref, same_ref, other_ref, e_ref):
    t = temperature(fetched(me_ref, h_ref), fetched(me_ref, s_ref), tab_ref[...])
    store(same_ref, other_ref, t)
    e_ref[0] = edge_rows(t)


def rate_of(t, halo_ref, crossed_ref, back_refs):
    wall = jnp.concatenate([spread(ref) for ref in back_refs] + [spread(crossed_ref)], axis=0)
    return wall + span_term(t, halo_ref[0])


def middle_kernel(chips, me_ref, h_ref, s_ref, tab_ref, same_ref, other_ref, halo_ref, crossed_ref, *refs):
    back_refs, (same2_ref, other2_ref, part_ref, e_ref) = refs[:chips], refs[chips:]
    h = fetched(me_ref, h_ref)
    t = jnp.concatenate([spread(same_ref), spread(other_ref)], axis=0)
    rate = rate_of(t, halo_ref, crossed_ref, back_refs)
    section = h + (time_step * gamma_one) * rate
    part_ref[...] = (h + (time_step * (gamma_one + zeta_two)) * rate).reshape(part_ref.shape)
    t2 = temperature(section, fetched(me_ref, s_ref), tab_ref[...])
    store(same2_ref, other2_ref, t2)
    e_ref[0] = edge_rows(t2)


def last_kernel(chips, me_ref, same_ref, other_ref, halo_ref, part_ref, crossed_ref, *refs):
    back_refs = refs[:chips]
    out_ref, state_ref = refs[-2:]
    t = jnp.concatenate([spread(same_ref), spread(other_ref)], axis=0)
    rate = rate_of(t, halo_ref, crossed_ref, back_refs)
    out = part_ref[...].reshape(t.shape) + (time_step * gamma_two) * rate
    chip, core = me_ref[0], me_ref[1]
    r = out_ref.shape[-2]
    for q in range(2):
        for p in range(chips):
            at = (q * chips + p) * r
            out_ref[chip ^ p, core ^ q, 0] = out[at:at + r]
            state_ref[chip ^ p, core ^ q, 0] = t[at:at + r]


def pair_kernel(same_ref, crossed_ref, *outs):
    for p, out in enumerate(outs, 1):
        out[0] = same_ref[p]
        out[1] = crossed_ref[p]


def gather_kernel(*refs):
    for p, ref in enumerate(refs[:-1]):
        refs[-1][p] = ref[0]


def split(x):
    hi = lax.reduce_precision(x, 8, 7).astype(BF16)
    return hi, (x - hi.astype(F32)).astype(BF16)


def apply_wall(hi, lo, x):
    x_hi, x_lo = split(x)
    dot = functools.partial(jnp.dot, preferred_element_type=F32)
    return dot(hi, x_hi) + (dot(hi, x_lo) + dot(lo, x_hi))


def wall_kernel(chips, me_ref, hi_ref, lo_ref, same_ref, crossed_ref, *refs):
    moved, outs, hold = refs[:chips - 1], refs[chips - 1:-1], refs[-1]
    n, m, r, z = hold.shape
    chip, core = me_ref[0], me_ref[1]
    for q in range(2):
        hold[chip * 2 + (core ^ q)] = (same_ref, crossed_ref)[q][0]
        for p in range(1, chips):
            hold[(chip ^ p) * 2 + (core ^ q)] = moved[p - 1][q]
    hi, lo = hi_ref[...], lo_ref[...]
    t = jnp.concatenate([hold[:, k].reshape(n * r, z) for k in range(m)], axis=1)
    g = apply_wall(hi, lo, t)
    w = apply_wall(hi, lo, conductance(t) * g)
    for k in range(m):
        hold[:, k] = w[:, k * z:(k + 1) * z].reshape(n, r, z)
    for q in range(2):
        for p in range(chips):
            outs[p][q] = hold[(chip ^ p) * 2 + (core ^ q)]


def params():
    return pltpu.CompilerParams(vmem_limit_bytes=VMEM_BYTES)


def on_device(heat_content, interval_index, wall_matrix, base_temp, enth_offset, slope, curvature):
    planes, r, z = heat_content.shape
    n = lax.axis_size("wall")
    spans = lax.axis_size("span")
    chips = n // 2
    own = planes // n
    chunks = next(k for k in CHUNKS if own % k == 0)
    m = own // chunks
    order = ORDER if chips == 8 else list(range(1, chips))
    index = lax.axis_index("wall")
    me = jnp.stack([index // 2, index % 2]).astype(jnp.int32)
    h = heat_content.reshape(chips, 2, own, r, z)
    s = interval_index.reshape(chips, 2, own, r, z)
    tables = jnp.stack([base_temp, enth_offset, slope, curvature])
    tables = jnp.pad(tables, ((0, 4), (0, z - tables.shape[1])))
    w_hi, w_lo = split(wall_matrix)

    half = jax.ShapeDtypeStruct((chips, m, r, z), F32)
    pair = jax.ShapeDtypeStruct((2, m, r, z), F32)
    both = jax.ShapeDtypeStruct((2, chips, m, r, z), F32)
    full = jax.ShapeDtypeStruct((chips, 2, own, r, z), F32)
    edges = jax.ShapeDtypeStruct((m, 8, n * r), F32)
    whole_spec = lambda c: pl.BlockSpec((chips, 2, 1, r, z), lambda i, me: (0, 0, c * m + i, 0, 0))
    half_spec = pl.BlockSpec((chips, 1, r, z), lambda i, me: (0, i, 0, 0))
    back_spec = pl.BlockSpec((1, 1, r, z), lambda i, me: (0, i, 0, 0))
    both_spec = pl.BlockSpec((2, chips, 1, r, z), lambda i, me: (0, 0, i, 0, 0))
    edge_spec = pl.BlockSpec((1, 8, n * r), lambda i, me: (i, 0, 0))
    table_spec = pl.BlockSpec(tables.shape, lambda i, me: (0, 0))
    hbm = pl.BlockSpec(memory_space=pl.ANY)
    cells = n * m * r * z

    def cost(ops, arrays, flops=0):
        return pl.CostEstimate(flops=1, bytes_accessed=1, transcendentals=0)

    def call(kernel, ins, outs, shapes, estimate, name, aliases={}, scratch=(), steps=m):
        grid = pltpu.PrefetchScalarGridSpec(
            num_scalar_prefetch=1, grid=(steps,), in_specs=ins, out_specs=outs, scratch_shapes=scratch
        )
        return pl.pallas_call(
            kernel, grid_spec=grid, out_shape=shapes, input_output_aliases=aliases,
            compiler_params=params(), cost_estimate=estimate, name=name,
        )

    def first(c, me):
        return call(
            first_kernel, [whole_spec(c), whole_spec(c), table_spec], [half_spec, half_spec, edge_spec],
            [half, half, edges], cost(100, 3), "first",
        )(me, h, s, tables)

    def middle(c, same, other, halo, crossed, back):
        return call(
            functools.partial(middle_kernel, chips),
            [whole_spec(c), whole_spec(c), table_spec, half_spec, half_spec, edge_spec, half_spec] + [back_spec] * chips,
            [half_spec, half_spec, both_spec, edge_spec], [half, half, both, edges], cost(140, 6), "middle",
        )(me, h, s, tables, same, other, halo, crossed, *back)

    def last(c, same, other, halo, part, crossed, back, outs):
        return call(
            functools.partial(last_kernel, chips),
            [half_spec, half_spec, edge_spec, both_spec, half_spec] + [back_spec] * chips + [hbm] * len(outs),
            [whole_spec(c)] * 2, [full] * 2, cost(40, 5), "last",
            {6 + chips + i: i for i in range(len(outs))},
        )(me, same, other, halo, part, crossed, *back, *outs)

    def block(shape, at=0):
        return pl.BlockSpec(shape, lambda i, me: (at,) + (0,) * (len(shape) - 1))

    def wall_operator(same, crossed, moved):
        return call(
            functools.partial(wall_kernel, chips),
            [block(w_hi.shape)] * 2 + [block((1, m, r, z))] * 2 + [block(pair.shape)] * (chips - 1),
            [block(pair.shape)] * chips, [pair] * chips, cost(20, 3, 12 * n * r * cells), "wall",
            scratch=[pltpu.VMEM((n, m, r, z), F32)], steps=1,
        )(me, w_hi, w_lo, same, crossed, *moved)

    def pairs(same, crossed):
        vmem = pl.BlockSpec(memory_space=pltpu.VMEM)
        return pl.pallas_call(
            pair_kernel, out_shape=[pair] * (chips - 1), in_specs=[vmem] * 2, out_specs=[vmem] * (chips - 1),
            compiler_params=params(), cost_estimate=cost(1, 2), name="pairs",
        )(same, crossed)

    def gather(back):
        return pl.pallas_call(
            gather_kernel, grid=(1,), out_shape=half,
            in_specs=[pl.BlockSpec((1, m, r, z), lambda i: (1, 0, 0, 0))] * chips,
            out_specs=pl.BlockSpec(half.shape, lambda i: (0, 0, 0, 0)),
            compiler_params=params(), cost_estimate=cost(1, 1), name="gather",
        )(*back)

    sent = []

    def after(x, tokens):
        return lax.optimization_barrier((x, *tokens))[0] if tokens else x

    def between_chips(arrays, places, tokens=()):
        moved = {}
        for p in (order[k] for k in places):
            x = after(arrays[p - 1], tuple(sent[-WINDOW:][:1] if len(sent) >= WINDOW else ()) + tuple(tokens))
            moved[p] = lax.ppermute(x, "wall", [(i, i ^ (2 * p)) for i in range(n)])
            sent.append(moved[p])
            tokens = ()
        return moved

    def between_cores(x):
        return lax.ppermute(x, "wall", [(i, i ^ 1) for i in range(n)])

    def neighbours(e):
        forward = [(i, (i + 1) % spans) for i in range(spans)]
        if spans == 2:
            return lax.ppermute(e, "span", forward)
        backward = [(target, source) for source, target in forward]
        up = lax.ppermute(e[:, 0:1], "span", backward)
        down = lax.ppermute(e[:, 1:2], "span", forward)
        return jnp.concatenate([up, down, jnp.zeros_like(e[:, 2:])], axis=1)

    chunk = [dict() for _ in range(chunks)]
    outs = ()

    def start_first(c, tokens):
        d = chunk[c]
        d["same"], d["other"], e = first(c, after(me, tokens))
        d["crossed"] = between_cores(d["other"])
        d["halo"] = neighbours(e)
        d["send"] = pairs(d["same"], d["crossed"])
        return d["same"]

    def produce(c, phase, tokens=()):
        nonlocal outs
        d = chunk[c]
        moved = [d["moved"][p] for p in range(1, chips)]
        if phase in (1, 3):
            w = wall_operator(d["same"], after(d["crossed"], tokens), moved)
            d["own"], d["send"] = w[0], w[1:]
            return w[0]
        back = [d["own"]] + moved
        crossed = after(between_cores(gather(back)), tokens)
        if phase == 2:
            d["same"], d["other"], d["part"], e = middle(c, d["same"], d["other"], d["halo"], crossed, back)
            d["crossed"] = between_cores(d["other"])
            d["halo"] = neighbours(e)
            d["send"] = pairs(d["same"], d["crossed"])
            return d["same"]
        outs = last(c, d["same"], d["other"], d["halo"], d["part"], crossed, back, outs)
        return outs[0]

    start_first(0, ())
    early = min(EARLY, len(order))
    for j in range(4 * chunks):
        phase, c = divmod(j, chunks)
        d = chunk[c]
        tokens = []
        d["moved"] = between_chips(d["send"], range(early))
        if j + 1 < chunks:
            tokens.append(start_first(j + 1, (d["send"][order[0] - 1],)))
        if j >= 1:
            before, k = divmod(j - 1, chunks)
            tokens.append(produce(k, before + 1))
        late = list(range(early, len(order)))
        d["moved"].update(between_chips(d["send"], late[:-1], tokens))
        d["moved"].update(between_chips(d["send"], late[-1:], (d["halo"],) if phase in (0, 2) else ()))
    produce(chunks - 1, 4)
    return outs[0].reshape(planes, r, z), outs[1].reshape(planes, r, z)


def solution(mesh):
    in_specs = (P(None, "wall", "span"), P(None, "wall", "span"), P(), P(), P(), P(), P())
    out_specs = (P(None, "wall", "span"), P(None, "wall", "span"))
    return jax.shard_map(
        on_device, mesh=mesh, in_specs=in_specs, out_specs=out_specs, check_vma=False
    )
```
